512 devices in a mesh: dp: 32 (over z, y_lo, core), tensor: 16 (over y_hi, x).
Axes of the slice: x: 4, y: 8 (y_hi: 4, y_lo: 2; y = y_hi * 2 + y_lo), z: 8, core: 2. Of those that a mesh axis runs over, the one named last changes fastest.
Arguments:
- hidden: bfloat16 [16384, 24576], P('dp', 'tensor'), may hold values from -6 to 6
- resid: bfloat16 [16384, 3072], P(('dp', 'tensor')), may hold values from -6 to 6
- down_w: bfloat16 [24576, 3072], P('tensor', 'dp'), may hold values from -0.0390625 to 0.0390625
- inputs: bfloat16 [16384, 1024], P('dp'), may hold values from -6 to 6
- gain: float32 [1024], replicated, may hold values from 0.25 to 1.75
- head: bfloat16 [1024, 3072], P(None, 'tensor'), may hold values from -0.1875 to 0.1875
Outputs:
- input_grad: bfloat16 [16384, 1024], P(('dp', 'tensor'))
- head_grad: float32 [1024, 3072], P(None, 'tensor')
The draws below stay inside these ranges and needn't reach their ends.
All inputs are finite; a program needn't handle non-finite values.
Results may differ from the reference program's by a relative error of at most 0.027.
Values may be sent and summed in bfloat16 or wider, within the bound.
No kernel may reach another device: no remote copies, remote signals or barrier semaphores. Data moves between devices by JAX's collectives and lax.ppermute only.
A program may use at most 64 MiB of HBM per device.

```python
import jax
import jax.numpy as jnp
from jax import lax

FF = 24576
DT = 3072
DS = 1024
TOK_DP = 512
TOKENS = 16384
N_TENSOR = 16


def strengthened(result, stream_key, source, target, shards_of, factor):
    owner, partner = [(jnp.arange(result.shape[axis_at]) // (result.shape[axis_at] // shards_of)).reshape([-1 if axis == axis_at else 1 for axis in range(result.ndim)]) for axis_at in (source, target)]
    chosen = jax.random.permutation(stream_key, shards_of)[partner]
    strong = (owner == chosen) | (owner == (partner + shards_of // 2) % shards_of)
    return jnp.where(strong, factor * result, result)


def block_scale(rng, extent, shards, smallest, largest):
    level = 1.0
    for dim, parts in shards:
        draws = jax.random.uniform(jax.random.fold_in(jax.random.fold_in(rng, 6), dim), (parts,), jnp.float32, smallest / len(shards), largest / len(shards))
        level = level * jnp.repeat(jnp.exp(draws), extent[dim] // parts).reshape((-1,) + (1,) * (len(extent) - 1 - dim))
    return level


def gaussian(stream_key, dims, spread, most, shards=(), dtype=jnp.bfloat16):
    array = jax.random.normal(stream_key, dims, jnp.float32) * spread
    if len(shards) > 0:
        array = block_scale(stream_key, dims, shards, -0.22, 0.18) * array
    return jnp.clip(array, min=-most, max=most).astype(dtype)


def heavy_noise(own_key, dims, width, reach, shards, heavy, held_as=jnp.bfloat16):
    result = width * jax.random.normal(own_key, dims, jnp.float32)
    if shards:
        result = result * block_scale(own_key, dims, shards, -0.22, 0.18)
    return jnp.clip(strengthened(result, jax.random.fold_in(own_key, 3), *heavy), -reach, reach).astype(held_as)


def setup_inputs(seed: int = 0) -> dict:
    key_list = jax.random.split(jax.random.key(seed), 7)
    return {
        "hidden": heavy_noise(key_list[0], (TOKENS, FF), 1.0, 6.0, ((0, 32), (1, 16)), (1, 0, 32, 2.75)),
        "resid": gaussian(key_list[1], (TOKENS, DT), 1.0, 6.0, ((0, 512),)),
        "down_w": gaussian(key_list[2], (FF, DT), FF ** -0.5, 0.0390625, ((0, 16), (1, 32))),
        "inputs": gaussian(key_list[3], (TOKENS, DS), 1.0, 6.0, ((0, 32),)),
        "gain": jnp.clip(1.0 + 0.15 * jax.random.normal(key_list[4], (DS,), jnp.float32), 0.25, 1.75),
        "head": gaussian(key_list[5], (DS, DT), DS ** -0.5, 0.1875, ((1, 16),)),
    }


def reference(hidden, resid, down_w, inputs, gain, head):
    block = FF // N_TENSOR
    teacher_sum = jnp.zeros((TOKENS, DT), jnp.float32)
    for index in range(N_TENSOR):
        part = jnp.dot(hidden[:, index * block:(index + 1) * block], down_w[index * block:(index + 1) * block], preferred_element_type=jnp.float32)
        teacher_sum = teacher_sum + lax.optimization_barrier(part.astype(jnp.bfloat16)).astype(jnp.float32)
    features = resid.astype(jnp.float32) + teacher_sum
    center = features - lax.optimization_barrier(jnp.mean(features, axis=1, keepdims=True))
    variance = lax.optimization_barrier(jnp.mean(center * center, axis=1, keepdims=True))
    target = (center * lax.rsqrt(variance + 1e-06)).astype(jnp.bfloat16)
    values = inputs.astype(jnp.float32)
    rms = jnp.sqrt(lax.optimization_barrier(jnp.mean(values * values, axis=1, keepdims=True)) + 1e-06)
    normed = (values / rms * gain).astype(jnp.bfloat16)
    pred = jnp.dot(normed, head, preferred_element_type=jnp.float32)
    delta = (pred - target.astype(jnp.float32)).astype(jnp.bfloat16)
    head_grad = lax.dot_general(normed, delta, (((0,), (0,)), ((), ())), preferred_element_type=jnp.float32) / TOK_DP
    cols = DT // N_TENSOR
    dnormed = jnp.zeros((TOKENS, DS), jnp.float32)
    for index in range(N_TENSOR):
        part = lax.dot_general(delta[:, index * cols:(index + 1) * cols], head[:, index * cols:(index + 1) * cols], (((1,), (1,)), ((), ())), preferred_element_type=jnp.float32)
        dnormed = dnormed + lax.optimization_barrier(part.astype(jnp.bfloat16)).astype(jnp.float32)
    scaled = gain * dnormed
    total = lax.optimization_barrier(jnp.sum(scaled * values, axis=1, keepdims=True))
    input_grad = scaled / rms - values * total / (DS * rms * rms * rms)
    return (input_grad.astype(jnp.bfloat16), head_grad)
```

```python
import jax
import jax.numpy as jnp
from jax import lax
from jax.sharding import Mesh, PartitionSpec as P

AXES = ("z", "yl", "c", "yh", "x")
SIZES = (8, 2, 2, 4, 4)
TENSOR = ("yh", "x")
SWAP = [(0, 1), (1, 0)]
F32 = jnp.float32
BF16 = jnp.bfloat16


def dot_nt(a, b):
    return lax.dot_general(a, b, (((1,), (1,)), ((), ())), preferred_element_type=F32)


def local(hidden, resid, down_w, inputs, gain, head):
    rows, depth = hidden.shape
    half = down_w.shape[1]
    width = inputs.shape[1]
    nz, nyh, nx = 8, 4, 4
    nt = nyh * nx
    own = rows // nt
    cols = nz * half
    yl = lax.axis_index("yl")
    core = lax.axis_index("c")
    mine = lax.axis_index(TENSOR)

    w = lax.all_gather(down_w.T, "z", axis=0, tiled=True)

    hidden_y = lax.ppermute(hidden, "yl", SWAP)
    hidden_c = lax.ppermute(hidden, "c", SWAP)
    hidden_yc = lax.ppermute(hidden_y, "c", SWAP)

    inputs_c = lax.ppermute(inputs, "c", SWAP)

    def norm(block):
        values = block.astype(F32)
        rms = jnp.sqrt(jnp.mean(values * values, axis=1, keepdims=True) + 1e-06)
        return (values / rms * gain).astype(BF16)

    def rows_of(block):
        return lax.dynamic_slice_in_dim(block, mine * own, own, 0)

    normed = norm(inputs)
    normed_c = norm(inputs_c)
    normed_own = jnp.concatenate([rows_of(normed), rows_of(normed_c)], axis=0)
    head_half = lax.dynamic_slice_in_dim(head.T, core * half, half, 0)
    head_y = lax.all_gather(head_half, "yh", axis=0)
    head_x = lax.all_to_all(
        jnp.broadcast_to(head_y[None], (nx,) + head_y.shape), "x", 0, 0, tiled=True
    )
    head_all = head_x.reshape(2, 2, nyh, half, width).transpose(1, 2, 0, 3, 4).reshape(2, cols, width)
    pred = jnp.stack([dot_nt(normed_own, head_all[0]), dot_nt(normed_own, head_all[1])])

    resid_parts = resid.reshape(own, nz, 2, 2, half)
    resid_keep = lax.dynamic_index_in_dim(resid_parts, core, 3, keepdims=False)
    resid_send = lax.dynamic_index_in_dim(resid_parts, 1 - core, 3, keepdims=False)
    resid_recv = lax.ppermute(resid_send, "c", SWAP)
    resid_own = jnp.stack([resid_keep, resid_recv]).transpose(3, 0, 1, 2, 4).reshape(2, 2 * own, cols)

    def partial(block):
        return dot_nt(block, w).astype(BF16).reshape(nyh, nx, own, cols)

    parts = jnp.stack(
        [
            jnp.stack([partial(hidden), partial(hidden_c)]),
            jnp.stack([partial(hidden_y), partial(hidden_yc)]),
        ]
    )
    parts = parts.transpose(3, 0, 2, 1, 4, 5)
    got_x = lax.all_to_all(parts, "x", 0, 0, tiled=True)
    sum_x = jnp.sum(got_x.astype(F32), axis=0).astype(BF16)
    sum_x = jnp.where(yl == 0, sum_x, sum_x[::-1])
    send_y = sum_x.transpose(1, 0, 2, 3, 4).reshape(2 * nyh, 2 * own, cols)
    got_y = lax.all_to_all(send_y, ("yh", "yl"), 0, 0, tiled=True)
    feats = jnp.sum(got_y.reshape(nyh, 2, 2 * own, cols).astype(F32), axis=0)
    feats = feats + resid_own.astype(F32)

    count = 2 * cols
    mean = jnp.mean(feats, axis=(0, 2))
    square = jnp.sum((feats - mean[None, :, None]) ** 2, axis=(0, 2))
    stats = jnp.stack([mean, square]).reshape(2, 2, own)
    other = lax.ppermute(stats, "c", SWAP)[:, ::-1].reshape(2, 2 * own)
    gap = mean - other[0]
    total_mean = 0.5 * (mean + other[0])
    variance = (square + other[1] + gap * gap * (0.5 * count)) / (2 * count)
    scale = lax.rsqrt(variance + 1e-06)
    target = ((feats - total_mean[None, :, None]) * scale[None, :, None]).astype(BF16)
    delta = (pred - target.astype(F32)).astype(BF16)

    send_t = delta.reshape(2, 2 * own, nz, half).transpose(2, 0, 1, 3).reshape(nt, 2 * own, half)
    got_t = lax.all_to_all(send_t, TENSOR, 0, 0, tiled=True)

    def grad(block, delta_rows):
        return lax.dot_general(
            block, delta_rows.reshape(rows, half), (((0,), (0,)), ((), ())), preferred_element_type=F32
        )

    head_part = (grad(normed, got_t[:, :own]) + grad(normed_c, got_t[:, own:])).astype(BF16)
    head_rows = width // (2 * nz)
    got_g = lax.all_to_all(head_part.reshape(2 * nz, head_rows, half), ("z", "yl"), 0, 0, tiled=True)
    head_sum = jnp.sum(got_g.astype(F32), axis=0).astype(BF16)
    all_g = lax.all_to_all(
        jnp.broadcast_to(head_sum[None], (2 * nz, head_rows, half)), ("z", "yl"), 0, 0, tiled=True
    ).reshape(width, half)
    other_g = lax.ppermute(all_g, "c", SWAP)
    left = jnp.where(core == 0, all_g, other_g)
    right = jnp.where(core == 0, other_g, all_g)
    head_grad = jnp.concatenate([left, right], axis=1).astype(F32) / rows

    dn = lax.dot_general(
        delta[0], head_all[0], (((1,), (0,)), ((), ())), preferred_element_type=F32
    ) + lax.dot_general(delta[1], head_all[1], (((1,), (0,)), ((), ())), preferred_element_type=F32)
    dnormed = dn[:own] + lax.ppermute(dn[own:].astype(BF16), "c", SWAP).astype(F32)
    values = rows_of(inputs).astype(F32)
    rms = jnp.sqrt(jnp.mean(values * values, axis=1, keepdims=True) + 1e-06)
    scaled = gain * dnormed
    total = jnp.sum(scaled * values, axis=1, keepdims=True)
    input_grad = scaled / rms - values * total / (width * rms * rms * rms)
    return input_grad.astype(BF16), head_grad


def solution(mesh):
    fine = Mesh(mesh.devices.reshape(SIZES), AXES)
    dp, tensor = ("z", "yl", "c"), ("yh", "x")
    in_specs = (P(dp, tensor), P(dp + tensor, None), P(tensor, dp), P(dp, None), P(), P(None, tensor))
    out_specs = (P(dp + tensor, None), P(None, tensor))
    return jax.shard_map(local, mesh=fine, in_specs=in_specs, out_specs=out_specs, check_vma=False)
```

```python
import functools

import jax
import jax.numpy as jnp
from jax import lax
from jax.experimental import pallas as pl
from jax.experimental.pallas import tpu as pltpu
from jax.sharding import Mesh, PartitionSpec as P

AXES = ("z", "yl", "c", "yh", "x")
SIZES = (8, 2, 2, 4, 4)
NZ, NYH, NX = 8, 4, 4
NT = NYH * NX
TENSOR = ("yh", "x")
REPLICA = ("z", "yl")
SWAP = [(0, 1), (1, 0)]
F32 = jnp.float32
BF16 = jnp.bfloat16
VMEM = pl.BlockSpec(memory_space=pltpu.VMEM)
SMEM = pl.BlockSpec(memory_space=pltpu.SMEM)
ANY = pl.BlockSpec(memory_space=pl.ANY)
PARAMS = pltpu.CompilerParams(vmem_limit_bytes=16 * 1024 * 1024)


def dot_nt(a, b):
    return lax.dot_general(a, b, (((1,), (1,)), ((), ())), preferred_element_type=F32)


def product_kernel(owners, own, core, other, both, w, mine, rest):
    depth = own.shape[-1]
    own_rows = own.shape[2]
    lhs = jnp.concatenate(
        [ref[...].reshape(NYH * own_rows, depth) for ref in (own, core, other, both)], axis=0
    )
    width = NYH * w.shape[2]
    rhs = w[...].reshape(width, depth)
    part = dot_nt(lhs, rhs).astype(BF16).reshape(2, 2, NYH, own_rows, width)
    for c in range(2):
        mine[0, :, c] = part[0, c]
        rest[0, :, c] = part[1, c]


def product(owners, blocks, w):
    count = owners.shape[0]
    rows, depth = blocks[0].shape
    own_rows = rows // NT
    half = w.shape[0] // NZ
    width = NYH * half
    block = pl.BlockSpec((NYH, 1, own_rows, depth), lambda i, j, o: (0, o[i], 0, 0))
    out = pl.BlockSpec((1, NYH, 2, own_rows, width), lambda i, j, o: (i, 0, 0, 0, j))
    shape = jax.ShapeDtypeStruct((count, NYH, 2, own_rows, 2 * width), BF16)
    return pl.pallas_call(
        product_kernel,
        grid_spec=pltpu.PrefetchScalarGridSpec(
            num_scalar_prefetch=1,
            grid=(count, 2),
            in_specs=[block] * 4
            + [pl.BlockSpec((NYH, 1, half, depth), lambda i, j, o: (0, j, 0, 0))],
            out_specs=[out, out],
        ),
        out_shape=[shape, shape],
        compiler_params=pltpu.CompilerParams(vmem_limit_bytes=56 * 1024 * 1024),
        cost_estimate=pl.CostEstimate(
            flops=2 * count * rows * 2 * width * depth,
            bytes_accessed=count * 5_000_000,
            transcendentals=0,
        ),
        name="product",
    )(
        owners,
        *[b.reshape(NYH, NX, own_rows, depth) for b in blocks],
        w.reshape(NYH, 2, half, depth),
    )


def relay_kernel(mine, rest, from_low, from_high, up, down):
    up[0] = (mine[0].astype(F32) + from_low[0].astype(F32)).astype(BF16)
    up[1] = rest[0]
    down[0] = mine[1]
    down[1] = (rest[1].astype(F32) + from_high[0].astype(F32)).astype(BF16)


def relay(mine, rest, from_low, from_high):
    _, _, _, own_rows, cols = mine.shape
    pair = pl.BlockSpec((2, 1, 2, own_rows, cols), lambda i: (0, i, 0, 0, 0))
    single = pl.BlockSpec((1, 1, 2, own_rows, cols), lambda i: (0, i, 0, 0, 0))
    shape = jax.ShapeDtypeStruct((2, NYH, 2, own_rows, cols), BF16)
    return pl.pallas_call(
        relay_kernel,
        grid=(NYH,),
        in_specs=[pair, pair, single, single],
        out_specs=[pair, pair],
        out_shape=[shape, shape],
        compiler_params=PARAMS,
        name="relay",
    )(mine, rest, from_low, from_high)


def sum_x_kernel(yl, mine, rest, low, high, out):
    for step, ref in enumerate((mine, rest)):
        total = ref[0].astype(F32) + low[step].astype(F32) + high[step].astype(F32)
        out[:, (yl[0] + step) % 2] = total.astype(BF16)


def sum_x(yl, mine, rest, low, high):
    _, _, _, own_rows, cols = mine.shape
    single = pl.BlockSpec((1, 1, 2, own_rows, cols), lambda i: (2, i, 0, 0, 0))
    pair = pl.BlockSpec((2, 1, 2, own_rows, cols), lambda i: (0, i, 0, 0, 0))
    return pl.pallas_call(
        sum_x_kernel,
        grid=(NYH,),
        in_specs=[SMEM, single, single, pair, pair],
        out_specs=pl.BlockSpec((1, 2, 2, own_rows, cols), lambda i: (i, 0, 0, 0, 0)),
        out_shape=jax.ShapeDtypeStruct((NYH, 2, 2, own_rows, cols), BF16),
        compiler_params=PARAMS,
        name="sum_x",
    )(yl, mine, rest, low, high)


def features_kernel(got, resid, feats, stats):
    half = resid.shape[1] // NT
    for x in range(NX):
        xh, xl = divmod(x, 2)
        lanes = slice(xh * NYH * half, (xh + 1) * NYH * half)
        total = got[0, xl, :, lanes].astype(F32)
        for src in range(1, NYH):
            total = total + got[src, xl, :, lanes].astype(F32)
        for yh in range(NYH):
            place = slice((yh * NX + x) * half, (yh * NX + x + 1) * half)
            feats[:, place] = total[:, yh * half : (yh + 1) * half] + resid[:, place].astype(F32)
    whole = feats[...]
    mean = jnp.mean(whole, axis=1, keepdims=True)
    square = jnp.sum((whole - mean) ** 2, axis=1, keepdims=True)
    stats[0] = jnp.broadcast_to(mean, stats.shape[1:])
    stats[1] = jnp.broadcast_to(square, stats.shape[1:])


def features(got, resid):
    rows, cols = resid.shape
    return pl.pallas_call(
        features_kernel,
        in_specs=[VMEM, VMEM],
        out_specs=[VMEM, VMEM],
        out_shape=[
            jax.ShapeDtypeStruct((rows, cols), F32),
            jax.ShapeDtypeStruct((2, rows, 128), F32),
        ],
        compiler_params=PARAMS,
        name="features",
    )(got, resid)


def delta_kernel(feats, mine, other, pred, delta, send):
    rows, count = feats.shape
    own = rows // 2
    mean_a, square_a = mine[0, :, :1], mine[1, :, :1]
    mean_b = jnp.concatenate([other[0, own:, :1], other[0, :own, :1]], axis=0)
    square_b = jnp.concatenate([other[1, own:, :1], other[1, :own, :1]], axis=0)
    gap = mean_a - mean_b
    mean = 0.5 * (mean_a + mean_b)
    variance = (square_a + square_b + gap * gap * (0.5 * count)) / (2 * count)
    scale = lax.rsqrt(variance + 1e-06)
    target = ((feats[...] - mean) * scale).astype(BF16)
    result = (pred[...] - target.astype(F32)).astype(BF16)
    delta[...] = result
    half = count // NT
    for t in range(NT):
        send[t] = result[:, t * half : (t + 1) * half]


def deltas(feats, mine, other, pred):
    rows, count = feats.shape
    return pl.pallas_call(
        delta_kernel,
        in_specs=[VMEM] * 4,
        out_specs=[VMEM] * 2,
        out_shape=[
            jax.ShapeDtypeStruct((rows, count), BF16),
            jax.ShapeDtypeStruct((NT, rows, count // NT), BF16),
        ],
        compiler_params=PARAMS,
        name="delta",
    )(feats, mine, other, pred)


def resid_kernel(core, resid, keep, send):
    half = resid.shape[1] // (2 * NT)
    for t in range(NT):
        start = 2 * half * t
        place = slice(t * half, (t + 1) * half)
        first = resid[:, start : start + half]
        second = resid[:, start + half : start + 2 * half]
        keep[:, place] = jnp.where(core[0] == 0, first, second)
        send[:, place] = jnp.where(core[0] == 0, second, first)


def resid_halves(resid, core):
    rows, cols = resid.shape
    shape = jax.ShapeDtypeStruct((rows, cols // 2), BF16)
    return pl.pallas_call(
        resid_kernel,
        in_specs=[SMEM, VMEM],
        out_specs=[VMEM] * 2,
        out_shape=[shape, shape],
        compiler_params=PARAMS,
        name="resid_halves",
    )(core, resid)


def norm_kernel(mine, inputs, other, gain, normed, owned):
    scale = gain[...]

    def norm(block):
        values = block.astype(F32)
        rms = jnp.sqrt(jnp.mean(values * values, axis=-1, keepdims=True) + 1e-06)
        return (values / rms * scale).astype(BF16)

    for c, ref in enumerate((inputs, other)):
        for t in range(NT):
            normed[t, c] = norm(ref[t])
    owned[...] = normed[mine[0]]


def norms(mine, inputs, other, gain):
    rows, width = inputs.shape
    own = rows // NT
    return pl.pallas_call(
        norm_kernel,
        in_specs=[SMEM] + [VMEM] * 3,
        out_specs=[VMEM] * 2,
        out_shape=[
            jax.ShapeDtypeStruct((NT, 2, own, width), BF16),
            jax.ShapeDtypeStruct((2, own, width), BF16),
        ],
        compiler_params=PARAMS,
        name="norms",
    )(mine, inputs.reshape(NT, own, width), other.reshape(NT, own, width), gain.reshape(1, width))


def grad_kernel(delta, normed, out, rows, sems):
    parts = sems.shape[0]
    size = rows.shape[0] // parts
    copies = [
        pltpu.make_async_copy(
            normed.at[pl.ds(i * size, size)], rows.at[pl.ds(i * size, size)], sems.at[i]
        )
        for i in range(parts)
    ]
    for copy in copies:
        copy.start()
    for copy in copies:
        copy.wait()
    part = lax.dot_general(
        delta[...], rows[...], (((0,), (0,)), ((), ())), preferred_element_type=F32
    ).astype(BF16)
    _, high, wide = out.shape
    across = part.shape[1] // wide
    for i in range(out.shape[0]):
        a, b = divmod(i, across)
        out[i] = part[a * high : (a + 1) * high, b * wide : (b + 1) * wide]


def grad_part(delta, normed):
    shape = (2 * NZ, delta.shape[1] // 2, normed.shape[1] // NZ)
    return pl.pallas_call(
        grad_kernel,
        in_specs=[VMEM, ANY],
        out_specs=VMEM,
        out_shape=jax.ShapeDtypeStruct(shape, BF16),
        scratch_shapes=[pltpu.VMEM(normed.shape, BF16), pltpu.SemaphoreType.DMA((8,))],
        compiler_params=PARAMS,
        name="grad_part",
    )(delta, normed)


def sum_grad_kernel(got, out):
    total = got[0].astype(F32)
    for i in range(1, got.shape[0]):
        total = total + got[i].astype(F32)
    out[...] = jnp.broadcast_to(total.astype(BF16)[None], out.shape)


def sum_grad(got):
    return pl.pallas_call(
        sum_grad_kernel,
        in_specs=[VMEM],
        out_specs=VMEM,
        out_shape=jax.ShapeDtypeStruct(got.shape, BF16),
        compiler_params=PARAMS,
        name="sum_grad",
    )(got)


def join_kernel(divisor, core, mine, other, out):
    pieces, high, wide = mine.shape
    half = out.shape[0] // 2
    across = out.shape[1] // wide
    for ref, start in ((mine, core[0] * half), (other, (1 - core[0]) * half)):
        for i in range(pieces):
            a, b = divmod(i, across)
            rows = pl.ds(pl.multiple_of(start + a * high, 16), high)
            out[rows, b * wide : (b + 1) * wide] = ref[i].astype(F32) / divisor


def join(mine, other, core, divisor):
    pieces, high, wide = mine.shape
    return pl.pallas_call(
        functools.partial(join_kernel, divisor),
        in_specs=[SMEM, VMEM, VMEM],
        out_specs=VMEM,
        out_shape=jax.ShapeDtypeStruct((4 * high, pieces * wide // 2), F32),
        compiler_params=PARAMS,
        name="join",
    )(core, mine, other)


def send_x(block, step):
    return lax.ppermute(block, "x", [(i, (i + step) % NX) for i in range(NX)])


def local(hidden, resid, down_w, inputs, gain, head):
    rows, depth = hidden.shape
    half = down_w.shape[1]
    width = inputs.shape[1]
    own = rows // NT
    cols = NZ * half
    yl = lax.axis_index("yl").astype(jnp.int32).reshape(1)
    core_id = lax.axis_index("c").astype(jnp.int32)
    core = core_id.reshape(1)
    mine = lax.axis_index(TENSOR)

    w = lax.all_gather(down_w.T, "z", axis=0, tiled=True)

    hidden_y = lax.ppermute(hidden, "yl", SWAP)
    hidden_c = lax.ppermute(hidden, "c", SWAP)
    inputs_c = lax.ppermute(inputs, "c", SWAP)
    head_half = lax.dynamic_slice_in_dim(head.T, core_id * half, half, 0)
    head_x = lax.all_to_all(
        jnp.broadcast_to(head_half[None], (NX, half, width)), "x", 0, 0, tiled=True
    )
    resid_keep, resid_send = resid_halves(resid, core)
    resid_own = jnp.concatenate([resid_keep, lax.ppermute(resid_send, "c", SWAP)], axis=0)
    normed, normed_own = norms(mine.astype(jnp.int32).reshape(1), inputs, inputs_c, gain)
    hidden_y, hidden_c, head_x, resid_own, normed, normed_own = lax.optimization_barrier(
        (hidden_y, hidden_c, head_x, resid_own, normed, normed_own)
    )
    hidden_yc = lax.ppermute(hidden_y, "c", SWAP)
    w, head_x = lax.optimization_barrier((w, head_x))
    head_all = lax.all_gather(head_x, "yh", axis=0).reshape(2 * cols, width)

    x = lax.axis_index("x").astype(jnp.int32)
    blocks = (hidden, hidden_c, hidden_y, hidden_yc)
    far_mine, far_rest = product(jnp.stack([(x + 2) % NX]), blocks, w)
    from_low = send_x(far_mine, 1)
    from_high = send_x(far_rest, -1)
    mine_parts, rest_parts = product(jnp.stack([(x + 1) % NX, (x + 3) % NX, x]), blocks, w)
    up, down = relay(mine_parts, rest_parts, from_low, from_high)
    low, high = send_x(up, 1), send_x(down, -1)

    send_y = sum_x(yl, mine_parts, rest_parts, low, high).reshape(2 * NYH, 2 * own, cols)
    got_y = lax.all_to_all(send_y, ("yh", "yl"), 0, 0, tiled=True)
    pred = dot_nt(normed_own.reshape(2 * own, width), head_all)
    feats, stats = features(got_y.reshape(NYH, 2, 2 * own, cols), resid_own)

    delta, send_t = deltas(feats, stats, lax.ppermute(stats, "c", SWAP), pred)

    got_t = lax.all_to_all(send_t, TENSOR, 0, 0, tiled=True)
    head_part = grad_part(got_t.reshape(2 * rows, half), normed.reshape(2 * rows, width))
    got_g = lax.all_to_all(head_part, REPLICA, 0, 0, tiled=True)
    all_g = lax.all_to_all(sum_grad(got_g), REPLICA, 0, 0, tiled=True)
    head_grad = join(all_g, lax.ppermute(all_g, "c", SWAP), core, float(rows)).T

    dn = jnp.dot(delta, head_all, preferred_element_type=F32)
    dnormed = dn[:own] + lax.ppermute(dn[own:].astype(BF16), "c", SWAP).astype(F32)
    values = lax.dynamic_slice_in_dim(inputs, mine * own, own, 0).astype(F32)
    rms = jnp.sqrt(jnp.mean(values * values, axis=1, keepdims=True) + 1e-06)
    scaled = gain * dnormed
    total = jnp.sum(scaled * values, axis=1, keepdims=True)
    input_grad = scaled / rms - values * total / (width * rms * rms * rms)
    return input_grad.astype(BF16), head_grad


def solution(mesh):
    fine = Mesh(mesh.devices.reshape(SIZES), AXES)
    dp, tensor = ("z", "yl", "c"), ("yh", "x")
    in_specs = (P(dp, tensor), P(dp + tensor, None), P(tensor, dp), P(dp, None), P(), P(None, tensor))
    out_specs = (P(dp + tensor, None), P(None, tensor))
    return jax.shard_map(local, mesh=fine, in_specs=in_specs, out_specs=out_specs, check_vma=False)
```

```python
import functools

import jax
import jax.numpy as jnp
from jax import lax
from jax.experimental import pallas as pl
from jax.experimental.pallas import tpu as pltpu
from jax.sharding import Mesh, PartitionSpec as P

AXES = ("z", "yl", "c", "yh", "x")
SIZES = (8, 2, 2, 4, 4)
NZ, NYH, NX = 8, 4, 4
NT = NYH * NX
TENSOR = ("yh", "x")
REPLICA = ("z", "yl")
SWAP = [(0, 1), (1, 0)]
F32 = jnp.float32
BF16 = jnp.bfloat16
VMEM = pl.BlockSpec(memory_space=pltpu.VMEM)
SMEM = pl.BlockSpec(memory_space=pltpu.SMEM)
ANY = pl.BlockSpec(memory_space=pl.ANY)
PARAMS = pltpu.CompilerParams(vmem_limit_bytes=16 * 1024 * 1024)


def dot_nt(a, b):
    return lax.dot_general(a, b, (((1,), (1,)), ((), ())), preferred_element_type=F32)


def product_kernel(owners, own, core, other, both, w, mine, rest):
    depth = own.shape[-1]
    own_rows = own.shape[2]
    lhs = jnp.concatenate(
        [ref[...].reshape(NYH * own_rows, depth) for ref in (own, core, other, both)], axis=0
    )
    width = NYH * w.shape[2]
    rhs = w[...].reshape(width, depth)
    part = dot_nt(lhs, rhs).astype(BF16).reshape(2, 2, NYH, own_rows, width)
    for c in range(2):
        mine[0, :, c] = part[0, c]
        rest[0, :, c] = part[1, c]


def product(owners, blocks, w):
    count = owners.shape[0]
    rows, depth = blocks[0].shape
    own_rows = rows // NT
    half = w.shape[0] // NZ
    width = NYH * half
    block = pl.BlockSpec((NYH, 1, own_rows, depth), lambda i, j, o: (0, o[i], 0, 0))
    out = pl.BlockSpec((1, NYH, 2, own_rows, width), lambda i, j, o: (i, 0, 0, 0, j))
    shape = jax.ShapeDtypeStruct((count, NYH, 2, own_rows, 2 * width), BF16)
    return pl.pallas_call(
        product_kernel,
        grid_spec=pltpu.PrefetchScalarGridSpec(
            num_scalar_prefetch=1,
            grid=(count, 2),
            in_specs=[block] * 4
            + [pl.BlockSpec((NYH, 1, half, depth), lambda i, j, o: (0, j, 0, 0))],
            out_specs=[out, out],
        ),
        out_shape=[shape, shape],
        compiler_params=pltpu.CompilerParams(vmem_limit_bytes=56 * 1024 * 1024),
        cost_estimate=pl.CostEstimate(
            flops=2 * count * rows * 2 * width * depth,
            bytes_accessed=count * 5_000_000,
            transcendentals=0,
        ),
        name="product",
    )(
        owners,
        *[b.reshape(NYH, NX, own_rows, depth) for b in blocks],
        w.reshape(NYH, 2, half, depth),
    )


def relay_kernel(mine, rest, from_low, from_high, up, down):
    up[0] = (mine[0].astype(F32) + from_low[0].astype(F32)).astype(BF16)
    up[1] = rest[0]
    down[0] = mine[1]
    down[1] = (rest[1].astype(F32) + from_high[0].astype(F32)).astype(BF16)


def relay(mine, rest, from_low, from_high):
    _, _, _, own_rows, cols = mine.shape
    pair = pl.BlockSpec((2, 1, 2, own_rows, cols), lambda i: (0, i, 0, 0, 0))
    single = pl.BlockSpec((1, 1, 2, own_rows, cols), lambda i: (0, i, 0, 0, 0))
    shape = jax.ShapeDtypeStruct((2, NYH, 2, own_rows, cols), BF16)
    return pl.pallas_call(
        relay_kernel,
        grid=(NYH,),
        in_specs=[pair, pair, single, single],
        out_specs=[pair, pair],
        out_shape=[shape, shape],
        compiler_params=PARAMS,
        name="relay",
    )(mine, rest, from_low, from_high)


def sum_x_kernel(yl, mine, rest, low, high, out):
    for step, ref in enumerate((mine, rest)):
        total = ref[0].astype(F32) + low[step].astype(F32) + high[step].astype(F32)
        out[:, (yl[0] + step) % 2] = total.astype(BF16)


def sum_x(yl, mine, rest, low, high):
    _, _, _, own_rows, cols = mine.shape
    single = pl.BlockSpec((1, 1, 2, own_rows, cols), lambda i: (2, i, 0, 0, 0))
    pair = pl.BlockSpec((2, 1, 2, own_rows, cols), lambda i: (0, i, 0, 0, 0))
    return pl.pallas_call(
        sum_x_kernel,
        grid=(NYH,),
        in_specs=[SMEM, single, single, pair, pair],
        out_specs=pl.BlockSpec((1, 2, 2, own_rows, cols), lambda i: (i, 0, 0, 0, 0)),
        out_shape=jax.ShapeDtypeStruct((NYH, 2, 2, own_rows, cols), BF16),
        compiler_params=PARAMS,
        name="sum_x",
    )(yl, mine, rest, low, high)


def features_kernel(got, resid, feats, stats):
    half = resid.shape[1] // NT
    for x in range(NX):
        xh, xl = divmod(x, 2)
        lanes = slice(xh * NYH * half, (xh + 1) * NYH * half)
        total = got[0, xl, :, lanes].astype(F32)
        for src in range(1, NYH):
            total = total + got[src, xl, :, lanes].astype(F32)
        for yh in range(NYH):
            place = slice((yh * NX + x) * half, (yh * NX + x + 1) * half)
            feats[:, place] = total[:, yh * half : (yh + 1) * half] + resid[:, place].astype(F32)
    whole = feats[...]
    mean = jnp.mean(whole, axis=1, keepdims=True)
    square = jnp.sum((whole - mean) ** 2, axis=1, keepdims=True)
    stats[0] = jnp.broadcast_to(mean, stats.shape[1:])
    stats[1] = jnp.broadcast_to(square, stats.shape[1:])


def features(got, resid):
    rows, cols = resid.shape
    return pl.pallas_call(
        features_kernel,
        in_specs=[VMEM, VMEM],
        out_specs=[VMEM, VMEM],
        out_shape=[
            jax.ShapeDtypeStruct((rows, cols), F32),
            jax.ShapeDtypeStruct((2, rows, 128), F32),
        ],
        compiler_params=PARAMS,
        name="features",
    )(got, resid)


def delta_kernel(feats, mine, other, pred, delta, send):
    rows, count = feats.shape
    own = rows // 2
    mean_a, square_a = mine[0, :, :1], mine[1, :, :1]
    mean_b = jnp.concatenate([other[0, own:, :1], other[0, :own, :1]], axis=0)
    square_b = jnp.concatenate([other[1, own:, :1], other[1, :own, :1]], axis=0)
    gap = mean_a - mean_b
    mean = 0.5 * (mean_a + mean_b)
    variance = (square_a + square_b + gap * gap * (0.5 * count)) / (2 * count)
    scale = lax.rsqrt(variance + 1e-06)
    target = ((feats[...] - mean) * scale).astype(BF16)
    result = (pred[...] - target.astype(F32)).astype(BF16)
    delta[...] = result
    half = count // NT
    for t in range(NT):
        send[t] = result[:, t * half : (t + 1) * half]


def deltas(feats, mine, other, pred):
    rows, count = feats.shape
    return pl.pallas_call(
        delta_kernel,
        in_specs=[VMEM] * 4,
        out_specs=[VMEM] * 2,
        out_shape=[
            jax.ShapeDtypeStruct((rows, count), BF16),
            jax.ShapeDtypeStruct((NT, rows, count // NT), BF16),
        ],
        compiler_params=PARAMS,
        name="delta",
    )(feats, mine, other, pred)


def resid_kernel(core, resid, keep, send):
    half = resid.shape[1] // (2 * NT)
    for t in range(NT):
        start = 2 * half * t
        place = slice(t * half, (t + 1) * half)
        first = resid[:, start : start + half]
        second = resid[:, start + half : start + 2 * half]
        keep[:, place] = jnp.where(core[0] == 0, first, second)
        send[:, place] = jnp.where(core[0] == 0, second, first)


def resid_halves(resid, core):
    rows, cols = resid.shape
    shape = jax.ShapeDtypeStruct((rows, cols // 2), BF16)
    return pl.pallas_call(
        resid_kernel,
        in_specs=[SMEM, VMEM],
        out_specs=[VMEM] * 2,
        out_shape=[shape, shape],
        compiler_params=PARAMS,
        name="resid_halves",
    )(core, resid)


def norm_kernel(mine, inputs, other, gain, normed, owned):
    scale = gain[...]

    def norm(block):
        values = block.astype(F32)
        rms = jnp.sqrt(jnp.mean(values * values, axis=-1, keepdims=True) + 1e-06)
        return (values / rms * scale).astype(BF16)

    for c, ref in enumerate((inputs, other)):
        for t in range(NT):
            normed[t, c] = norm(ref[t])
    owned[...] = normed[mine[0]]


def norms(mine, inputs, other, gain):
    rows, width = inputs.shape
    own = rows // NT
    return pl.pallas_call(
        norm_kernel,
        in_specs=[SMEM] + [VMEM] * 3,
        out_specs=[VMEM] * 2,
        out_shape=[
            jax.ShapeDtypeStruct((NT, 2, own, width), BF16),
            jax.ShapeDtypeStruct((2, own, width), BF16),
        ],
        compiler_params=PARAMS,
        name="norms",
    )(mine, inputs.reshape(NT, own, width), other.reshape(NT, own, width), gain.reshape(1, width))


def grad_kernel(delta, normed, out, rows, sems):
    parts = sems.shape[0]
    size = rows.shape[0] // parts
    copies = [
        pltpu.make_async_copy(
            normed.at[pl.ds(i * size, size)], rows.at[pl.ds(i * size, size)], sems.at[i]
        )
        for i in range(parts)
    ]
    for copy in copies:
        copy.start()
    for copy in copies:
        copy.wait()
    part = lax.dot_general(
        delta[...], rows[...], (((0,), (0,)), ((), ())), preferred_element_type=F32
    ).astype(BF16)
    _, high, wide = out.shape
    across = part.shape[1] // wide
    for i in range(out.shape[0]):
        a, b = divmod(i, across)
        out[i] = part[a * high : (a + 1) * high, b * wide : (b + 1) * wide]


def grad_part(delta, normed):
    shape = (2 * NZ, delta.shape[1] // 2, normed.shape[1] // NZ)
    return pl.pallas_call(
        grad_kernel,
        in_specs=[VMEM, ANY],
        out_specs=VMEM,
        out_shape=jax.ShapeDtypeStruct(shape, BF16),
        scratch_shapes=[pltpu.VMEM(normed.shape, BF16), pltpu.SemaphoreType.DMA((8,))],
        compiler_params=PARAMS,
        name="grad_part",
    )(delta, normed)


def sum_grad_kernel(got, out):
    total = got[0].astype(F32)
    for i in range(1, got.shape[0]):
        total = total + got[i].astype(F32)
    out[...] = jnp.broadcast_to(total.astype(BF16)[None], out.shape)


def sum_grad(got):
    return pl.pallas_call(
        sum_grad_kernel,
        in_specs=[VMEM],
        out_specs=VMEM,
        out_shape=jax.ShapeDtypeStruct(got.shape, BF16),
        compiler_params=PARAMS,
        name="sum_grad",
    )(got)


def join_kernel(divisor, core, mine, other, out):
    pieces, high, wide = mine.shape
    half = out.shape[0] // 2
    across = out.shape[1] // wide
    for ref, start in ((mine, core[0] * half), (other, (1 - core[0]) * half)):
        for i in range(pieces):
            a, b = divmod(i, across)
            rows = pl.ds(pl.multiple_of(start + a * high, 16), high)
            out[rows, b * wide : (b + 1) * wide] = ref[i].astype(F32) / divisor


def join(mine, other, core, divisor):
    pieces, high, wide = mine.shape
    return pl.pallas_call(
        functools.partial(join_kernel, divisor),
        in_specs=[SMEM, VMEM, VMEM],
        out_specs=VMEM,
        out_shape=jax.ShapeDtypeStruct((4 * high, pieces * wide // 2), F32),
        compiler_params=PARAMS,
        name="join",
    )(core, mine, other)


def send_x(block, step):
    return lax.ppermute(block, "x", [(i, (i + step) % NX) for i in range(NX)])


def local(hidden, resid, down_w, inputs, gain, head):
    rows, depth = hidden.shape
    half = down_w.shape[1]
    width = inputs.shape[1]
    own = rows // NT
    cols = NZ * half
    yl = lax.axis_index("yl").astype(jnp.int32).reshape(1)
    core_id = lax.axis_index("c").astype(jnp.int32)
    core = core_id.reshape(1)
    mine = lax.axis_index(TENSOR)

    w = lax.all_gather(down_w.T, "z", axis=0, tiled=True)

    hidden_y = lax.ppermute(hidden, "yl", SWAP)
    hidden_c = lax.ppermute(hidden, "c", SWAP)
    inputs_c = lax.ppermute(inputs, "c", SWAP)
    head_half = lax.dynamic_slice_in_dim(head.T, core_id * half, half, 0)
    head_x = lax.all_to_all(
        jnp.broadcast_to(head_half[None], (NX, half, width)), "x", 0, 0, tiled=True
    )
    resid_keep, resid_send = resid_halves(resid, core)
    resid_own = jnp.concatenate([resid_keep, lax.ppermute(resid_send, "c", SWAP)], axis=0)
    normed, normed_own = norms(mine.astype(jnp.int32).reshape(1), inputs, inputs_c, gain)
    hidden_y, hidden_c, head_x, resid_own, normed, normed_own = lax.optimization_barrier(
        (hidden_y, hidden_c, head_x, resid_own, normed, normed_own)
    )
    hidden_yc = lax.ppermute(hidden_y, "c", SWAP)
    w, head_x = lax.optimization_barrier((w, head_x))
    head_all = lax.all_gather(head_x, "yh", axis=0).reshape(2 * cols, width)

    x = lax.axis_index("x").astype(jnp.int32)
    blocks = (hidden, hidden_c, hidden_y, hidden_yc)
    far_mine, far_rest = product(jnp.stack([(x + 2) % NX]), blocks, w)
    from_low = send_x(far_mine, 1)
    from_high = send_x(far_rest, -1)
    mine_parts, rest_parts = product(jnp.stack([(x + 1) % NX, (x + 3) % NX, x]), blocks, w)
    up, down = relay(mine_parts, rest_parts, from_low, from_high)
    low, high = send_x(up, 1), send_x(down, -1)

    send_y = sum_x(yl, mine_parts, rest_parts, low, high).reshape(2 * NYH, 2 * own, cols)
    got_y = lax.all_to_all(send_y, ("yh", "yl"), 0, 0, tiled=True)
    pred = dot_nt(normed_own.reshape(2 * own, width), head_all)
    got_y, pred = lax.optimization_barrier((got_y, pred))
    feats, stats = features(got_y.reshape(NYH, 2, 2 * own, cols), resid_own)

    delta, send_t = deltas(feats, stats, lax.ppermute(stats, "c", SWAP), pred)

    got_t = lax.all_to_all(send_t, TENSOR, 0, 0, tiled=True)
    head_part = grad_part(got_t.reshape(2 * rows, half), normed.reshape(2 * rows, width))
    got_g = lax.all_to_all(head_part, REPLICA, 0, 0, tiled=True)
    all_g = lax.all_to_all(sum_grad(got_g), REPLICA, 0, 0, tiled=True)
    head_grad = join(all_g, lax.ppermute(all_g, "c", SWAP), core, float(rows)).T

    dn = jnp.dot(delta, head_all, preferred_element_type=F32)
    dnormed = dn[:own] + lax.ppermute(dn[own:].astype(BF16), "c", SWAP).astype(F32)
    values = lax.dynamic_slice_in_dim(inputs, mine * own, own, 0).astype(F32)
    rms = jnp.sqrt(jnp.mean(values * values, axis=1, keepdims=True) + 1e-06)
    scaled = gain * dnormed
    total = jnp.sum(scaled * values, axis=1, keepdims=True)
    input_grad = scaled / rms - values * total / (width * rms * rms * rms)
    return input_grad.astype(BF16), head_grad


def solution(mesh):
    fine = Mesh(mesh.devices.reshape(SIZES), AXES)
    dp, tensor = ("z", "yl", "c"), ("yh", "x")
    in_specs = (P(dp, tensor), P(dp + tensor, None), P(tensor, dp), P(dp, None), P(), P(None, tensor))
    out_specs = (P(dp + tensor, None), P(None, tensor))
    return jax.shard_map(local, mesh=fine, in_specs=in_specs, out_specs=out_specs, check_vma=False)
```

```python
import functools

import jax
import jax.numpy as jnp
from jax import lax
from jax.experimental import pallas as pl
from jax.experimental.pallas import tpu as pltpu
from jax.sharding import Mesh, PartitionSpec as P

AXES = ("z", "yl", "c", "yh", "x")
SIZES = (8, 2, 2, 4, 4)
NZ, NYH, NX = 8, 4, 4
NT = NYH * NX
TENSOR = ("yh", "x")
REPLICA = ("z", "yl")
SWAP = [(0, 1), (1, 0)]
F32 = jnp.float32
BF16 = jnp.bfloat16
VMEM = pl.BlockSpec(memory_space=pltpu.VMEM)
SMEM = pl.BlockSpec(memory_space=pltpu.SMEM)
ANY = pl.BlockSpec(memory_space=pl.ANY)
PARAMS = pltpu.CompilerParams(vmem_limit_bytes=16 * 1024 * 1024)


def dot_nt(a, b):
    return lax.dot_general(a, b, (((1,), (1,)), ((), ())), preferred_element_type=F32)


def product_kernel(owners, own, core, other, both, w, mine, rest):
    depth = own.shape[-1]
    own_rows = own.shape[2]
    lhs = jnp.concatenate(
        [ref[...].reshape(NYH * own_rows, depth) for ref in (own, core, other, both)], axis=0
    )
    width = NYH * w.shape[2]
    rhs = w[...].reshape(width, depth)
    part = dot_nt(lhs, rhs).astype(BF16).reshape(2, 2, NYH, own_rows, width)
    for c in range(2):
        mine[0, :, c] = part[0, c]
        rest[0, :, c] = part[1, c]


def product(owners, blocks, w):
    count = owners.shape[0]
    rows, depth = blocks[0].shape
    own_rows = rows // NT
    half = w.shape[0] // NZ
    width = NYH * half
    block = pl.BlockSpec((NYH, 1, own_rows, depth), lambda i, j, o: (0, o[i], 0, 0))
    out = pl.BlockSpec((1, NYH, 2, own_rows, width), lambda i, j, o: (i, 0, 0, 0, j))
    shape = jax.ShapeDtypeStruct((count, NYH, 2, own_rows, 2 * width), BF16)
    return pl.pallas_call(
        product_kernel,
        grid_spec=pltpu.PrefetchScalarGridSpec(
            num_scalar_prefetch=1,
            grid=(count, 2),
            in_specs=[block] * 4
            + [pl.BlockSpec((NYH, 1, half, depth), lambda i, j, o: (0, j, 0, 0))],
            out_specs=[out, out],
        ),
        out_shape=[shape, shape],
        compiler_params=pltpu.CompilerParams(vmem_limit_bytes=56 * 1024 * 1024),
        cost_estimate=pl.CostEstimate(
            flops=2 * count * rows * 2 * width * depth,
            bytes_accessed=count * 5_000_000,
            transcendentals=0,
        ),
        name="product",
    )(
        owners,
        *[b.reshape(NYH, NX, own_rows, depth) for b in blocks],
        w.reshape(NYH, 2, half, depth),
    )


def relay_kernel(mine, rest, from_low, from_high, up, down):
    up[0] = (mine[0].astype(F32) + from_low[0].astype(F32)).astype(BF16)
    up[1] = rest[0]
    down[0] = mine[1]
    down[1] = (rest[1].astype(F32) + from_high[0].astype(F32)).astype(BF16)


def relay(mine, rest, from_low, from_high):
    _, _, _, own_rows, cols = mine.shape
    pair = pl.BlockSpec((2, 1, 2, own_rows, cols), lambda i: (0, i, 0, 0, 0))
    single = pl.BlockSpec((1, 1, 2, own_rows, cols), lambda i: (0, i, 0, 0, 0))
    shape = jax.ShapeDtypeStruct((2, NYH, 2, own_rows, cols), BF16)
    return pl.pallas_call(
        relay_kernel,
        grid=(NYH,),
        in_specs=[pair, pair, single, single],
        out_specs=[pair, pair],
        out_shape=[shape, shape],
        compiler_params=PARAMS,
        name="relay",
    )(mine, rest, from_low, from_high)


def sum_x_kernel(yl, mine, rest, low, high, out):
    for step, ref in enumerate((mine, rest)):
        total = ref[0].astype(F32) + low[step].astype(F32) + high[step].astype(F32)
        out[:, (yl[0] + step) % 2] = total.astype(BF16)


def sum_x(yl, mine, rest, low, high):
    _, _, _, own_rows, cols = mine.shape
    single = pl.BlockSpec((1, 1, 2, own_rows, cols), lambda i: (2, i, 0, 0, 0))
    pair = pl.BlockSpec((2, 1, 2, own_rows, cols), lambda i: (0, i, 0, 0, 0))
    return pl.pallas_call(
        sum_x_kernel,
        grid=(NYH,),
        in_specs=[SMEM, single, single, pair, pair],
        out_specs=pl.BlockSpec((1, 2, 2, own_rows, cols), lambda i: (i, 0, 0, 0, 0)),
        out_shape=jax.ShapeDtypeStruct((NYH, 2, 2, own_rows, cols), BF16),
        compiler_params=PARAMS,
        name="sum_x",
    )(yl, mine, rest, low, high)


def features_kernel(got, resid, feats, stats):
    half = resid.shape[1] // NT
    for x in range(NX):
        xh, xl = divmod(x, 2)
        lanes = slice(xh * NYH * half, (xh + 1) * NYH * half)
        total = got[0, xl, :, lanes].astype(F32)
        for src in range(1, NYH):
            total = total + got[src, xl, :, lanes].astype(F32)
        for yh in range(NYH):
            place = slice((yh * NX + x) * half, (yh * NX + x + 1) * half)
            feats[:, place] = total[:, yh * half : (yh + 1) * half] + resid[:, place].astype(F32)
    whole = feats[...]
    mean = jnp.mean(whole, axis=1, keepdims=True)
    square = jnp.sum((whole - mean) ** 2, axis=1, keepdims=True)
    stats[0] = jnp.broadcast_to(mean, stats.shape[1:])
    stats[1] = jnp.broadcast_to(square, stats.shape[1:])


def features(got, resid):
    rows, cols = resid.shape
    return pl.pallas_call(
        features_kernel,
        in_specs=[VMEM, VMEM],
        out_specs=[VMEM, VMEM],
        out_shape=[
            jax.ShapeDtypeStruct((rows, cols), F32),
            jax.ShapeDtypeStruct((2, rows, 128), F32),
        ],
        compiler_params=PARAMS,
        name="features",
    )(got, resid)


def delta_kernel(feats, mine, other, pred, delta, send):
    rows, count = feats.shape
    own = rows // 2
    mean_a, square_a = mine[0, :, :1], mine[1, :, :1]
    mean_b = jnp.concatenate([other[0, own:, :1], other[0, :own, :1]], axis=0)
    square_b = jnp.concatenate([other[1, own:, :1], other[1, :own, :1]], axis=0)
    gap = mean_a - mean_b
    mean = 0.5 * (mean_a + mean_b)
    variance = (square_a + square_b + gap * gap * (0.5 * count)) / (2 * count)
    scale = lax.rsqrt(variance + 1e-06)
    target = ((feats[...] - mean) * scale).astype(BF16)
    result = (pred[...] - target.astype(F32)).astype(BF16)
    delta[...] = result
    half = count // NT
    for t in range(NT):
        send[t] = result[:, t * half : (t + 1) * half]


def deltas(feats, mine, other, pred):
    rows, count = feats.shape
    return pl.pallas_call(
        delta_kernel,
        in_specs=[VMEM] * 4,
        out_specs=[VMEM] * 2,
        out_shape=[
            jax.ShapeDtypeStruct((rows, count), BF16),
            jax.ShapeDtypeStruct((NT, rows, count // NT), BF16),
        ],
        compiler_params=PARAMS,
        name="delta",
    )(feats, mine, other, pred)


def resid_kernel(core, resid, keep, send):
    half = resid.shape[1] // (2 * NT)
    for t in range(NT):
        start = 2 * half * t
        place = slice(t * half, (t + 1) * half)
        first = resid[:, start : start + half]
        second = resid[:, start + half : start + 2 * half]
        keep[:, place] = jnp.where(core[0] == 0, first, second)
        send[:, place] = jnp.where(core[0] == 0, second, first)


def resid_halves(resid, core):
    rows, cols = resid.shape
    shape = jax.ShapeDtypeStruct((rows, cols // 2), BF16)
    return pl.pallas_call(
        resid_kernel,
        in_specs=[SMEM, VMEM],
        out_specs=[VMEM] * 2,
        out_shape=[shape, shape],
        compiler_params=PARAMS,
        name="resid_halves",
    )(core, resid)


def norm_kernel(mine, inputs, other, gain, normed, owned):
    scale = gain[...]

    def norm(block):
        values = block.astype(F32)
        rms = jnp.sqrt(jnp.mean(values * values, axis=-1, keepdims=True) + 1e-06)
        return (values / rms * scale).astype(BF16)

    for c, ref in enumerate((inputs, other)):
        for t in range(NT):
            normed[t, c] = norm(ref[t])
    owned[...] = normed[mine[0]]


def norms(mine, inputs, other, gain):
    rows, width = inputs.shape
    own = rows // NT
    return pl.pallas_call(
        norm_kernel,
        in_specs=[SMEM] + [VMEM] * 3,
        out_specs=[VMEM] * 2,
        out_shape=[
            jax.ShapeDtypeStruct((NT, 2, own, width), BF16),
            jax.ShapeDtypeStruct((2, own, width), BF16),
        ],
        compiler_params=PARAMS,
        name="norms",
    )(mine, inputs.reshape(NT, own, width), other.reshape(NT, own, width), gain.reshape(1, width))


def grad_kernel(delta, normed, out, rows, sems):
    parts = sems.shape[0]
    size = rows.shape[0] // parts
    copies = [
        pltpu.make_async_copy(
            normed.at[pl.ds(i * size, size)], rows.at[pl.ds(i * size, size)], sems.at[i]
        )
        for i in range(parts)
    ]
    for copy in copies:
        copy.start()
    for copy in copies:
        copy.wait()
    part = lax.dot_general(
        delta[...], rows[...], (((0,), (0,)), ((), ())), preferred_element_type=F32
    ).astype(BF16)
    _, high, wide = out.shape
    across = part.shape[1] // wide
    for i in range(out.shape[0]):
        a, b = divmod(i, across)
        out[i] = part[a * high : (a + 1) * high, b * wide : (b + 1) * wide]


def grad_part(delta, normed):
    shape = (2 * NZ, delta.shape[1] // 2, normed.shape[1] // NZ)
    return pl.pallas_call(
        grad_kernel,
        in_specs=[VMEM, ANY],
        out_specs=VMEM,
        out_shape=jax.ShapeDtypeStruct(shape, BF16),
        scratch_shapes=[pltpu.VMEM(normed.shape, BF16), pltpu.SemaphoreType.DMA((8,))],
        compiler_params=PARAMS,
        name="grad_part",
    )(delta, normed)


def sum_grad_kernel(got, out):
    total = got[0].astype(F32)
    for i in range(1, got.shape[0]):
        total = total + got[i].astype(F32)
    out[...] = jnp.broadcast_to(total.astype(BF16)[None], out.shape)


def sum_grad(got):
    return pl.pallas_call(
        sum_grad_kernel,
        in_specs=[VMEM],
        out_specs=VMEM,
        out_shape=jax.ShapeDtypeStruct(got.shape, BF16),
        compiler_params=PARAMS,
        name="sum_grad",
    )(got)


def join_kernel(divisor, core, mine, other, out):
    pieces, high, wide = mine.shape
    half = out.shape[0] // 2
    across = out.shape[1] // wide
    for ref, start in ((mine, core[0] * half), (other, (1 - core[0]) * half)):
        for i in range(pieces):
            a, b = divmod(i, across)
            rows = pl.ds(pl.multiple_of(start + a * high, 16), high)
            out[rows, b * wide : (b + 1) * wide] = ref[i].astype(F32) / divisor


def join(mine, other, core, divisor):
    pieces, high, wide = mine.shape
    return pl.pallas_call(
        functools.partial(join_kernel, divisor),
        in_specs=[SMEM, VMEM, VMEM],
        out_specs=VMEM,
        out_shape=jax.ShapeDtypeStruct((4 * high, pieces * wide // 2), F32),
        compiler_params=PARAMS,
        name="join",
    )(core, mine, other)


def send_x(block, step):
    return lax.ppermute(block, "x", [(i, (i + step) % NX) for i in range(NX)])


def local(hidden, resid, down_w, inputs, gain, head):
    rows, depth = hidden.shape
    half = down_w.shape[1]
    width = inputs.shape[1]
    own = rows // NT
    cols = NZ * half
    yl = lax.axis_index("yl").astype(jnp.int32).reshape(1)
    core_id = lax.axis_index("c").astype(jnp.int32)
    core = core_id.reshape(1)
    mine = lax.axis_index(TENSOR)

    w = lax.all_gather(down_w.T, "z", axis=0, tiled=True)

    hidden_y = lax.ppermute(hidden, "yl", SWAP)
    hidden_c = lax.ppermute(hidden, "c", SWAP)
    inputs_c = lax.ppermute(inputs, "c", SWAP)
    head_half = lax.dynamic_slice_in_dim(head.T, core_id * half, half, 0)
    head_x = lax.all_to_all(
        jnp.broadcast_to(head_half[None], (NX, half, width)), "x", 0, 0, tiled=True
    )
    resid_keep, resid_send = resid_halves(resid, core)
    resid_own = jnp.concatenate([resid_keep, lax.ppermute(resid_send, "c", SWAP)], axis=0)
    normed, normed_own = norms(mine.astype(jnp.int32).reshape(1), inputs, inputs_c, gain)
    hidden_y, hidden_c, head_x, resid_own, normed, normed_own = lax.optimization_barrier(
        (hidden_y, hidden_c, head_x, resid_own, normed, normed_own)
    )
    hidden_yc = lax.ppermute(hidden_y, "c", SWAP)
    w, head_x, hidden_yc = lax.optimization_barrier((w, head_x, hidden_yc))
    head_all = lax.all_gather(head_x, "yh", axis=0).reshape(2 * cols, width)

    x = lax.axis_index("x").astype(jnp.int32)
    blocks = (hidden, hidden_c, hidden_y, hidden_yc)
    far_mine, far_rest = product(jnp.stack([(x + 2) % NX]), blocks, w)
    from_low = send_x(far_mine, 1)
    from_high = send_x(far_rest, -1)
    mine_parts, rest_parts = product(jnp.stack([(x + 1) % NX, (x + 3) % NX, x]), blocks, w)
    up, down = relay(mine_parts, rest_parts, from_low, from_high)
    low, high = send_x(up, 1), send_x(down, -1)

    send_y = sum_x(yl, mine_parts, rest_parts, low, high).reshape(2 * NYH, 2 * own, cols)
    got_y = lax.all_to_all(send_y, ("yh", "yl"), 0, 0, tiled=True)
    pred = dot_nt(normed_own.reshape(2 * own, width), head_all)
    got_y, pred = lax.optimization_barrier((got_y, pred))
    feats, stats = features(got_y.reshape(NYH, 2, 2 * own, cols), resid_own)

    delta, send_t = deltas(feats, stats, lax.ppermute(stats, "c", SWAP), pred)

    got_t = lax.all_to_all(send_t, TENSOR, 0, 0, tiled=True)
    head_part = grad_part(got_t.reshape(2 * rows, half), normed.reshape(2 * rows, width))
    got_g = lax.all_to_all(head_part, REPLICA, 0, 0, tiled=True)
    all_g = lax.all_to_all(sum_grad(got_g), REPLICA, 0, 0, tiled=True)
    head_grad = join(all_g, lax.ppermute(all_g, "c", SWAP), core, float(rows)).T

    dn = jnp.dot(delta, head_all, preferred_element_type=F32)
    dnormed = dn[:own] + lax.ppermute(dn[own:].astype(BF16), "c", SWAP).astype(F32)
    values = lax.dynamic_slice_in_dim(inputs, mine * own, own, 0).astype(F32)
    rms = jnp.sqrt(jnp.mean(values * values, axis=1, keepdims=True) + 1e-06)
    scaled = gain * dnormed
    total = jnp.sum(scaled * values, axis=1, keepdims=True)
    input_grad = scaled / rms - values * total / (width * rms * rms * rms)
    return input_grad.astype(BF16), head_grad


def solution(mesh):
    fine = Mesh(mesh.devices.reshape(SIZES), AXES)
    dp, tensor = ("z", "yl", "c"), ("yh", "x")
    in_specs = (P(dp, tensor), P(dp + tensor, None), P(tensor, dp), P(dp, None), P(), P(None, tensor))
    out_specs = (P(dp + tensor, None), P(None, tensor))
    return jax.shard_map(local, mesh=fine, in_specs=in_specs, out_specs=out_specs, check_vma=False)
```
